32 devices in a mesh: req: 8 (over z, y), tp: 4 (over x, core).
Axes of the slice: x: 2, y: 2, z: 4, core: 2. Of those that a mesh axis runs over, the one named last changes fastest.
Arguments:
- hidden: bfloat16 [8192, 2560], P('req'), may hold values from -6 to 6
- segments: int32 [8, 1024], P('req'), may hold values from 0 to 7, never falling along the last dimension, each value on 1 to 512 neighbouring positions
- send_order: int32 [8, 1024], P('req'), may hold values from 0 to 1023, each once within a row
- page_table: int32 [8, 64], replicated, may hold values from 0 to 511, as said below
- norm_gain: bfloat16 [2560], replicated, may hold values from 0.5 to 1.5
- w_query: bfloat16 [2560, 2560], P(None, 'tp'), may hold values from -0.125 to 0.125
- w_key: bfloat16 [2560, 640], P(None, 'tp'), may hold values from -0.125 to 0.125
- w_value: bfloat16 [2560, 640], P(None, 'tp'), may hold values from -0.125 to 0.125
- w_output: bfloat16 [2560, 2560], P('tp'), may hold values from -0.125 to 0.125
Outputs:
- hidden_out: bfloat16 [8192, 2560], P('req', 'tp')
- kv_cache: bfloat16 [512, 16, 8, 160], P('req', None, 'tp')
The draws below stay inside these ranges and needn't reach their ends.
Inputs may be any that keep to these rules, and one draw needn't show every extreme that they name: `send_order`: each row lists every local token once; the token in send position j goes to the device of req index j // 128. `segments`: never falling along a block; a prompt lies within one block. `page_table`: every cache page appears once in the whole table; page q belongs to req index q // 64, and each row names exactly 8 pages of each req index.
All inputs are finite; a program needn't handle non-finite values.
Results may differ from the reference program's by a relative error of at most 0.006.
Values may be sent and summed in bfloat16 or wider, within the bound.
A program may use at most 128 MiB of HBM per device.

```python
import math
import jax
import jax.numpy as jnp
import numpy as np
from jax import lax

D = 2560
QH = 32
KVH = 8
HD = 80
TOK_DEV = 1024
LONGEST = 512
PAGE = 16
GROUPS = 8
HEAD_GROUPS = 4
TOKENS = 8192
SEGS = 8
PAGES_DEV = 64


def draw_page_table(key, part):
    owner_key, slot_key = jax.random.split(key)
    per_owner = PAGES_DEV // GROUPS
    owner_list = jnp.repeat(jnp.arange(GROUPS, dtype=jnp.int32), per_owner)
    slot_list = jnp.arange(PAGES_DEV, dtype=jnp.int32)

    def shuffle_owners(row_key):
        return jax.random.permutation(row_key, owner_list)

    def shuffle_slots(row_key):
        return jax.random.permutation(row_key, slot_list)
    owners = jax.vmap(shuffle_owners)(jax.random.split(owner_key, GROUPS))
    owner_hits = (owners[:, :, None] == jnp.arange(GROUPS, dtype=jnp.int32)[None, None, :]).astype(jnp.int32)
    arrival = jnp.sum(jnp.cumsum(owner_hits, axis=1) * owner_hits, axis=-1) - 1
    slot_perm = jax.vmap(shuffle_slots)(jax.random.split(slot_key, GROUPS))
    source = jnp.arange(GROUPS, dtype=jnp.int32)[:, None]
    slots = slot_perm[owners, source * per_owner + arrival]
    return (owners * PAGES_DEV + slots).astype(jnp.int32)


def block_scale(stream_key, extent, pieces, least, top_value):
    def one(dim, shards_of):
        heights = jax.random.uniform(jax.random.fold_in(jax.random.fold_in(stream_key, 6), dim), (shards_of,), jnp.float32, least / len(pieces), top_value / len(pieces))
        return jnp.repeat(jnp.exp(heights), extent[dim] // shards_of).reshape((-1,) + (1,) * (len(extent) - dim - 1))

    gain = one(*pieces[0])
    for cut in pieces[1:]:
        gain = gain * one(*cut)
    return gain


def length_profile(number_of, total, most, skew):
    loads = [(1 << 20) // math.isqrt(rank ** skew) + 1 for rank in range(2, number_of + 1)]
    spare, given = total - most - (number_of - 1), [1] * (number_of - 1)
    while spare > 0:
        movable = [i for i in range(number_of - 1) if given[i] < most]
        whole, left = sum([loads[i] for i in movable]), spare
        for i in movable:
            more = min(most - given[i], max(1, left * loads[i] // whole), spare)
            given[i] = given[i] + more
            spare = spare - more
    return np.array([most] + given)


def ragged_sizes(own_key, count, total, limit, lean):
    if count == 2:
        one = jax.random.randint(own_key, (), max(1, total - limit), min(limit, total - 1) + 1)
        return jnp.stack([one, total - one])
    sizes = jnp.asarray(length_profile(count, total, limit, lean), jnp.int32)
    twos = (count - 1) // 2
    giver, sink = sizes[1:1 + 2 * twos:2], sizes[2:2 + 2 * twos:2]
    room = jnp.minimum(giver - 1, limit - sink)
    moved = jax.random.randint(jax.random.fold_in(own_key, 1), (twos,), 0, 1 << 20) % (room + 1)
    sizes = sizes.at[1:1 + 2 * twos:2].set(giver - moved).at[2:2 + 2 * twos:2].set(sink + moved)
    return sizes[jax.random.permutation(jax.random.fold_in(own_key, 2), count)]


def gaussian(own_key, shape, deviation, limit, cuts=(), kind=jnp.bfloat16):
    level = block_scale(own_key, shape, cuts, -0.22, 0.18) if cuts else 1.0
    entries = jax.random.normal(own_key, shape, jnp.float32) * deviation * level
    return jnp.minimum(jnp.maximum(entries, -limit), limit).astype(kind)


def setup_inputs(seed: int = 0) -> dict:
    keys = jax.random.split(jax.random.key(seed), 10)
    return {
        "hidden": gaussian(keys[0], (TOKENS, D), 1.0, 6.0, ((0, 8),)),
        "segments": jax.vmap(lambda own: jnp.searchsorted(jnp.cumsum(ragged_sizes(own, SEGS, TOK_DEV, LONGEST, 2)), jnp.arange(TOK_DEV), side="right"))(jax.random.split(keys[1], GROUPS)).reshape((GROUPS, TOK_DEV)).astype(jnp.int32),
        "send_order": jax.vmap(lambda own: jax.random.permutation(own, TOK_DEV))(jax.random.split(keys[2], GROUPS)).reshape((GROUPS, TOK_DEV)).astype(jnp.int32),
        "page_table": draw_page_table(jax.random.fold_in(keys[9], 71), 0),
        "norm_gain": jnp.clip(1.0 + 0.1 * jax.random.normal(keys[4], (D,), jnp.float32), 0.5, 1.5).astype(jnp.bfloat16),
        "w_query": gaussian(keys[5], (D, QH * HD), D ** -0.5, 0.125, ((1, 4),)),
        "w_key": gaussian(keys[6], (D, KVH * HD), D ** -0.5, 0.125, ((1, 4),)),
        "w_value": gaussian(keys[7], (D, KVH * HD), D ** -0.5, 0.125, ((1, 4),)),
        "w_output": gaussian(keys[8], (QH * HD, D), (QH * HD) ** -0.5, 0.125, ((0, 4),)),
    }


eps_norm = 1e-05
rope_base = 1000000.0

def to_bf16(array_in):
    return lax.optimization_barrier(array_in.astype(jnp.bfloat16))

def rotate_half(vectors):
    half_width = vectors.shape[-1] // 2
    return jnp.concatenate([-vectors[..., half_width:], vectors[..., :half_width]], axis=-1)

def rope_tables(segment_row):
    length = segment_row.shape[0]
    places = jnp.arange(length, dtype=jnp.int32)
    earlier = jnp.concatenate([segment_row[:1] - 1, segment_row[:-1]])
    starts = jnp.where(segment_row != earlier, places, 0).astype(jnp.int32)
    first_index = lax.cummax(starts, axis=0)
    position = (places - first_index).astype(jnp.float32)
    frequency = rope_base ** (-jnp.arange(0, HD, 2, dtype=jnp.float32) / HD)
    angles = position[:, None] * frequency[None, :]
    angles = jnp.concatenate([angles, angles], axis=-1)
    return (jnp.cos(angles), jnp.sin(angles))

def layer_block(dealt_block, segment_row, norm_gain, w_query, w_key, w_value, w_output):
    length = dealt_block.shape[0]
    widened = dealt_block.astype(jnp.float32)
    inverse_rms = lax.rsqrt(lax.optimization_barrier(jnp.mean(widened * widened, axis=-1, keepdims=True)) + eps_norm)
    normed = (widened * inverse_rms * norm_gain.astype(jnp.float32)).astype(jnp.bfloat16)
    query_raw = jnp.dot(normed, w_query, preferred_element_type=jnp.float32).reshape(length, QH, HD)
    key_raw = jnp.dot(normed, w_key, preferred_element_type=jnp.float32).reshape(length, KVH, HD)
    value_heads = to_bf16(jnp.dot(normed, w_value, preferred_element_type=jnp.float32)).reshape(length, KVH, HD)
    cosine_table, sine_table = rope_tables(segment_row)
    query_heads = to_bf16(query_raw * cosine_table[:, None, :] + rotate_half(query_raw) * sine_table[:, None, :])
    key_heads = to_bf16(key_raw * cosine_table[:, None, :] + rotate_half(key_raw) * sine_table[:, None, :])
    head_ratio = QH // KVH
    grouped = query_heads.reshape(length, KVH, head_ratio, HD).astype(jnp.float32)
    scores = jnp.einsum('qgrd,kgd->grqk', grouped, key_heads.astype(jnp.float32)) / math.sqrt(HD)
    places = jnp.arange(length, dtype=jnp.int32)
    allowed = (segment_row[:, None] == segment_row[None, :]) & (places[None, :] <= places[:, None])
    probs = jnp.where(allowed[None, None], jnp.exp(scores), 0.0)
    total_mass = lax.optimization_barrier(jnp.sum(probs, axis=-1))
    numerator = jnp.einsum('grqk,kgd->qgrd', to_bf16(probs).astype(jnp.float32), value_heads.astype(jnp.float32))
    attended = (numerator / jnp.transpose(total_mass, (2, 0, 1))[..., None]).astype(jnp.bfloat16)
    group_cols = QH * HD // HEAD_GROUPS
    split_attended = to_bf16(attended.reshape(length, HEAD_GROUPS, group_cols).astype(jnp.float32))
    split_output = w_output.reshape(HEAD_GROUPS, group_cols, D).astype(jnp.float32)
    partial_value = jnp.einsum('tgc,gcd->gtd', split_attended.astype(jnp.float32), split_output)
    partial_value = to_bf16(partial_value).astype(jnp.float32)
    block_out = (widened + lax.optimization_barrier(jnp.sum(partial_value, axis=0))).astype(jnp.bfloat16)
    kv_rows = jnp.concatenate([key_heads, value_heads], axis=-1)
    return (block_out, kv_rows)

def reference(hidden, segments, send_order, page_table, norm_gain, w_query, w_key, w_value, w_output):
    groups = segments.shape[0]
    length = segments.shape[1]
    per_pair = length // groups
    anchor = jnp.arange(groups, dtype=jnp.int32)[:, None] * length + send_order.astype(jnp.int32)
    anchor = jnp.transpose(anchor.reshape(groups, groups, per_pair), (1, 0, 2)).reshape(-1).astype(jnp.int32)
    dealt_rows = hidden[anchor].reshape(groups, length, D)

    def one_block(inputs):
        return layer_block(inputs[0], inputs[1], norm_gain, w_query, w_key, w_value, w_output)
    block_out, kv_rows = lax.map(one_block, (dealt_rows, segments))
    hidden_out = jnp.zeros_like(hidden).at[anchor].set(block_out.reshape(-1, D))
    page_blocks = kv_rows.reshape(groups * PAGES_DEV, PAGE, KVH, 2 * HD)
    kv_cache = jnp.zeros_like(page_blocks).at[page_table.reshape(-1).astype(jnp.int32)].set(page_blocks)
    return (hidden_out, kv_cache)
```

```python
import math

import jax
import jax.numpy as jnp
from jax import lax
from jax.sharding import PartitionSpec as P

HD = 80
PAGE = 16
LONGEST = 512

eps_norm = 1e-05
rope_base = 1000000.0
F32 = jnp.float32
BF16 = jnp.bfloat16


def rotate_half(vectors):
    half_width = vectors.shape[-1] // 2
    return jnp.concatenate([-vectors[..., half_width:], vectors[..., :half_width]], axis=-1)


def rope_tables(segment_row):
    length = segment_row.shape[0]
    places = jnp.arange(length, dtype=jnp.int32)
    first_index = jnp.sum((segment_row[None, :] < segment_row[:, None]).astype(jnp.int32), axis=1)
    position = (places - first_index).astype(F32)
    frequency = rope_base ** (-jnp.arange(0, HD, 2, dtype=F32) / HD)
    angles = position[:, None] * frequency[None, :]
    angles = jnp.concatenate([angles, angles], axis=-1)
    return (jnp.cos(angles), jnp.sin(angles))


def attention(query_heads, key_heads, value_heads, segment_row):
    length = query_heads.shape[0]
    kv_local = key_heads.shape[1]
    head_ratio = query_heads.shape[1] // kv_local
    tile = min(256, length)
    places = jnp.arange(length, dtype=jnp.int32)
    pieces_out = []
    for low in range(0, length, tile):
        high = low + tile
        first = max(0, low - LONGEST)
        grouped = query_heads[low:high].reshape(tile, kv_local, head_ratio, HD)
        scores = jnp.einsum(
            "qgrd,kgd->grqk", grouped, key_heads[first:high], preferred_element_type=F32
        ) / math.sqrt(HD)
        allowed = (segment_row[low:high, None] == segment_row[None, first:high]) & (
            places[None, first:high] <= places[low:high, None]
        )
        probs = jnp.where(allowed[None, None], jnp.exp(scores), 0.0)
        total_mass = jnp.sum(probs, axis=-1)
        numerator = jnp.einsum(
            "grqk,kgd->qgrd", probs.astype(BF16), value_heads[first:high],
            preferred_element_type=F32,
        )
        pieces_out.append(numerator / jnp.transpose(total_mass, (2, 0, 1))[..., None])
    return jnp.concatenate(pieces_out, axis=0)


def one_hot_rows(index, count):
    return (index[:, None] == jnp.arange(count, dtype=jnp.int32)[None, :]).astype(BF16)


def local(hidden, segments, send_order, page_table, norm_gain, w_query, w_key, w_value, w_output):
    groups = lax.axis_size("req")
    tp_count = lax.axis_size("tp")
    length, width = hidden.shape
    share = length // groups
    part = width // tp_count
    cores = 2 if tp_count % 2 == 0 else 1
    xs = tp_count // cores
    tp_place = lax.axis_index("tp")
    my_x, my_core = tp_place // cores, tp_place % cores
    order_grid = send_order[0].reshape(groups, share)
    segment_row = segments[0]

    def piece(k, e):
        return lax.rem(my_x + k, xs) * cores + (my_core ^ e)

    def from_x(array, k):
        pairs = [
            (((x + k) % xs) * cores + c, x * cores + c) for x in range(xs) for c in range(cores)
        ]
        return lax.ppermute(array, "tp", pairs)

    def from_core(array):
        pairs = [(x * cores + (c ^ 1), x * cores + c) for x in range(xs) for c in range(cores)]
        return lax.ppermute(array, "tp", pairs)

    own_core = [piece(k, 0) for k in range(xs)]
    all_pieces = own_core + ([piece(k, 1) for k in range(xs)] if cores == 2 else [])

    widened = hidden.astype(F32)
    inverse_rms = lax.rsqrt(jnp.mean(widened * widened, axis=-1, keepdims=True) + eps_norm)

    def normed_columns(p):
        columns = lax.dynamic_slice_in_dim(hidden, p * part, part, 1).astype(F32)
        gain = lax.dynamic_slice_in_dim(norm_gain, p * part, part, 0).astype(F32)
        return (columns * inverse_rms * gain).astype(BF16)

    normed_own = [normed_columns(p) for p in own_core]

    cut = max(1, (share * 5 // 8) // 16) * 16 if share > 16 else share
    cuts = [(0, cut), (cut, share)] if cut < share else [(0, share)]

    def deal(columns, low, high):
        sent = jnp.dot(
            one_hot_rows(order_grid[:, low:high].reshape(-1), length), columns,
            preferred_element_type=F32,
        ).astype(BF16)
        return lax.all_to_all(sent, "req", split_axis=0, concat_axis=0, tiled=True)

    weights = jnp.concatenate([w_query, w_key, w_value], axis=1)
    weights = jnp.concatenate(
        [lax.dynamic_slice_in_dim(weights, p * part, part, 0) for p in all_pieces], axis=0
    )
    out_weights = [lax.dynamic_slice_in_dim(w_output, p * part, part, 1) for p in all_pieces]
    out_keep = jnp.concatenate(out_weights[:xs], axis=1)
    out_send = jnp.concatenate(out_weights[xs:], axis=1) if cores == 2 else None

    raw_parts = []
    for number, (low, high) in enumerate(cuts):
        if number == 0:
            mine = deal(normed_own[0], low, high)
            mine = jnp.concatenate([mine] + [from_x(mine, k) for k in range(1, xs)], axis=1)
        else:
            mine = deal(jnp.concatenate(normed_own, axis=1), low, high)
        half = mine.shape[1]
        raw = jnp.dot(mine, weights[:half], preferred_element_type=F32)
        if cores == 2:
            other = from_core(mine)
            raw = raw + jnp.dot(other, weights[half:], preferred_element_type=F32)
        raw_parts.append(raw.reshape(groups, high - low, -1))
    raw = jnp.concatenate(raw_parts, axis=1).reshape(length, -1)

    q_width, k_width = w_query.shape[1], w_key.shape[1]
    heads_local, kv_local = q_width // HD, k_width // HD
    query_raw = raw[:, :q_width].reshape(length, heads_local, HD)
    key_raw = raw[:, q_width : q_width + k_width].reshape(length, kv_local, HD)
    value_heads = raw[:, q_width + k_width :].astype(BF16).reshape(length, kv_local, HD)
    cosine_table, sine_table = rope_tables(segment_row)
    query_heads = (
        query_raw * cosine_table[:, None, :] + rotate_half(query_raw) * sine_table[:, None, :]
    ).astype(BF16)
    key_heads = (
        key_raw * cosine_table[:, None, :] + rotate_half(key_raw) * sine_table[:, None, :]
    ).astype(BF16)
    attended = attention(query_heads, key_heads, value_heads, segment_row)
    attended = attended.astype(BF16).reshape(groups, share, q_width)

    steps = 2 if share % 32 == 0 else 1
    total = lax.dynamic_slice_in_dim(hidden, tp_place * part, part, 1).astype(F32)
    for step in range(steps):
        low, high = step * share // steps, (step + 1) * share // steps
        rows = attended[:, low:high].reshape(-1, q_width)
        if cores == 2:
            given = jnp.dot(rows, out_send, preferred_element_type=F32).astype(BF16)
            came = from_core(given)
            kept = jnp.dot(rows, out_keep, preferred_element_type=F32)
            kept = kept + came.astype(F32)
        else:
            kept = jnp.dot(rows, out_keep, preferred_element_type=F32)
        summed = kept[:, :part]
        for k in range(1, xs):
            leaving = kept[:, k * part : (k + 1) * part].astype(BF16)
            summed = summed + from_x(leaving, xs - k).astype(F32)
        returned = lax.all_to_all(
            summed.astype(BF16), "req", split_axis=0, concat_axis=0, tiled=True
        )
        back = one_hot_rows(order_grid[:, low:high].reshape(-1), length)
        total = total + lax.dot_general(
            back, returned, (((0,), (0,)), ((), ())), preferred_element_type=F32
        )
    hidden_out = total.astype(BF16)

    pages_dev = length // PAGE
    per_owner = pages_dev // groups
    my_req = lax.axis_index("req")
    owners = page_table // pages_dev
    numbers = jnp.arange(pages_dev, dtype=jnp.int32)
    earlier = (owners[:, None, :] == owners[:, :, None]) & (numbers[None, :] < numbers[:, None])
    rank = jnp.sum(earlier.astype(jnp.int32), axis=-1)
    my_slots = lax.dynamic_slice_in_dim(owners * per_owner + rank, my_req, 1, 0)[0]
    kv_rows = jnp.concatenate([key_heads, value_heads], axis=-1)
    page_rows = kv_rows.reshape(pages_dev, PAGE * kv_local * 2 * HD)
    page_rows = jnp.dot(
        (my_slots[None, :] == numbers[:, None]).astype(BF16), page_rows,
        preferred_element_type=F32,
    ).astype(BF16)
    arrived = lax.all_to_all(page_rows, "req", split_axis=0, concat_axis=0, tiled=True)
    slot_here = jnp.where(
        owners == my_req, jnp.arange(groups, dtype=jnp.int32)[:, None] * per_owner + rank, -1
    ).reshape(-1)
    target = (page_table % pages_dev).reshape(-1)
    hit = (slot_here[:, None] == numbers[None, :]).astype(jnp.int32)
    slot_target = jnp.sum(hit * target[:, None], axis=0)
    place = (slot_target[None, :] == numbers[:, None]).astype(BF16)
    kv_cache = jnp.dot(place, arrived, preferred_element_type=F32).astype(BF16)
    return (hidden_out, kv_cache.reshape(pages_dev, PAGE, kv_local, 2 * HD))


def solution(mesh):
    return jax.shard_map(
        local,
        mesh=mesh,
        in_specs=(
            P("req", None),
            P("req", None),
            P("req", None),
            P(),
            P(),
            P(None, "tp"),
            P(None, "tp"),
            P(None, "tp"),
            P("tp", None),
        ),
        out_specs=(P("req", "tp"), P("req", None, "tp", None)),
        check_vma=False,
    )
```

```python
import functools
import math

import jax
import jax.numpy as jnp
from jax import lax
from jax.experimental import pallas as pl
from jax.experimental.pallas import tpu as pltpu
from jax.sharding import PartitionSpec as P

HD = 80
PAGE = 16
LONGEST = 512

eps_norm = 1e-05
rope_base = 1000000.0
F32 = jnp.float32
BF16 = jnp.bfloat16


LANES = 128


def padded_halves(array):
    rows = array.shape[0]
    split = array.reshape(rows, -1, 2, HD // 2)
    return jnp.pad(split, ((0, 0), (0, 0), (0, 0), (0, (LANES - HD) // 2))).reshape(rows, -1)


def padded_heads(array, axis):
    shape = array.shape
    split = array.reshape(shape[:axis] + (-1, HD) + shape[axis + 1 :])
    widths = [(0, 0)] * split.ndim
    widths[axis + 1] = (0, LANES - HD)
    return jnp.pad(split, widths).reshape(shape[:axis] + (-1,) + shape[axis + 1 :])


def rope_tables(segment_row):
    length = segment_row.shape[0]
    places = jnp.arange(length, dtype=jnp.int32)
    first_index = jnp.sum((segment_row[None, :] < segment_row[:, None]).astype(jnp.int32), axis=1)
    position = (places - first_index).astype(F32)
    frequency = rope_base ** (-jnp.arange(0, HD, 2, dtype=F32) / HD)
    angles = position[:, None] * frequency[None, :]
    cosine, sine = jnp.cos(angles), jnp.sin(angles)
    cosine = padded_halves(jnp.concatenate([cosine, cosine], axis=-1))
    sine = padded_halves(jnp.concatenate([-sine, sine], axis=-1))
    return cosine, sine, first_index


def attention_kernel(cuts, groups, heads, kv, steps, *refs):
    raw_refs, refs = refs[: len(cuts)], refs[len(cuts) :]
    cos_ref, sin_ref, first_ref = refs[:3]
    out_refs, refs = refs[3 : 3 + steps], refs[3 + steps :]
    key_ref, value_ref, query_scr, value_scr = refs
    share = cuts[-1][1]
    length = groups * share
    scale = math.log2(math.e) / math.sqrt(HD)

    for (low, high), raw_ref in zip(cuts, raw_refs):
        size = high - low

        @pl.loop(0, groups)
        def _(g):
            here = pl.ds(pl.multiple_of(g * size, 16), size)
            there = pl.ds(pl.multiple_of(g * share + low, 16), size)
            cosine, sine = cos_ref[there, :], sin_ref[there, :]
            for h in range(heads + kv):
                x = raw_ref[here, h * LANES : (h + 1) * LANES]
                turned = x * cosine + pltpu.roll(x, LANES // 2, 1) * sine
                if h < heads:
                    query_scr[there, h * LANES : (h + 1) * LANES] = turned.astype(BF16)
                else:
                    at = (h - heads) * LANES
                    key_ref[there, at : at + LANES] = turned.astype(BF16)
            lane = lax.broadcasted_iota(jnp.int32, (size, LANES), 1)
            for h in range(kv):
                at = (heads + kv + h) * LANES
                x = raw_ref[here, at : at + LANES]
                value_ref[there, h * LANES : (h + 1) * LANES] = x.astype(BF16)
                value_scr[there, h * LANES : (h + 1) * LANES] = jnp.where(
                    lane == HD, 1.0, x
                ).astype(BF16)

    tile = 256 if length % 256 == 0 else length
    ratio = heads // kv
    for low in range(0, length, tile):
        high = low + tile
        start = max(0, low - LONGEST)
        keys = high - start
        key_place = start + lax.broadcasted_iota(jnp.int32, (tile, keys), 1)
        query_place = low + lax.broadcasted_iota(jnp.int32, (tile, keys), 0)
        allowed = (key_place >= first_ref[low:high, :]) & (key_place <= query_place)

        @pl.loop(0, heads)
        def _(h):
            mine = pl.ds(pl.multiple_of(h * LANES, LANES), LANES)
            shared = pl.ds(pl.multiple_of((h // ratio) * LANES, LANES), LANES)
            scores = lax.dot_general(
                query_scr[low:high, mine], key_ref[start:high, shared],
                (((1,), (1,)), ((), ())), preferred_element_type=F32,
            )
            probs = jnp.where(allowed, jnp.exp2(scores * scale), 0.0).astype(BF16)
            sums = jnp.dot(probs, value_scr[start:high, shared], preferred_element_type=F32)
            done = (sums / sums[:, HD : HD + 1]).astype(BF16)
            run = share // steps
            for block in range(tile // run):
                g, step = divmod(low // run + block, steps)
                out_refs[step][g * run : (g + 1) * run, mine] = done[block * run : (block + 1) * run]


def attention(raw_parts, cuts, groups, heads, kv, steps, tables):
    cosine, sine, first_index = tables
    length = groups * cuts[-1][1]
    shapes = [jax.ShapeDtypeStruct((length // steps, heads * LANES), BF16)] * steps
    shapes += [jax.ShapeDtypeStruct((length, kv * LANES), BF16)] * 2
    whole = pl.BlockSpec(memory_space=pltpu.VMEM)
    outs = pl.pallas_call(
        functools.partial(attention_kernel, cuts, groups, heads, kv, steps),
        out_shape=shapes,
        in_specs=[whole] * (len(cuts) + 3),
        out_specs=[whole] * len(shapes),
        scratch_shapes=[
            pltpu.VMEM((length, heads * LANES), BF16),
            pltpu.VMEM((length, kv * LANES), BF16),
        ],
        compiler_params=pltpu.CompilerParams(vmem_limit_bytes=40 * 2**20),
        cost_estimate=pl.CostEstimate(
            flops=4 * length * 640 * heads * LANES, bytes_accessed=10 * 2**20,
            transcendentals=length * 640 * heads,
        ),
    )(*raw_parts, cosine, sine, first_index[:, None])
    return outs[:steps], outs[steps], outs[steps + 1]


def one_hot_rows(index, count):
    return (index[:, None] == jnp.arange(count, dtype=jnp.int32)[None, :]).astype(BF16)


def local(hidden, segments, send_order, page_table, norm_gain, w_query, w_key, w_value, w_output):
    groups = lax.axis_size("req")
    tp_count = lax.axis_size("tp")
    length, width = hidden.shape
    share = length // groups
    part = width // tp_count
    cores = 2 if tp_count % 2 == 0 else 1
    xs = tp_count // cores
    tp_place = lax.axis_index("tp")
    my_x, my_core = tp_place // cores, tp_place % cores
    order_grid = send_order[0].reshape(groups, share)
    segment_row = segments[0]

    def piece(k, e):
        return lax.rem(my_x + k, xs) * cores + (my_core ^ e)

    def from_x(array, k):
        pairs = [
            (((x + k) % xs) * cores + c, x * cores + c) for x in range(xs) for c in range(cores)
        ]
        return lax.ppermute(array, "tp", pairs)

    def from_core(array):
        pairs = [(x * cores + (c ^ 1), x * cores + c) for x in range(xs) for c in range(cores)]
        return lax.ppermute(array, "tp", pairs)

    own_core = [piece(k, 0) for k in range(xs)]
    all_pieces = own_core + ([piece(k, 1) for k in range(xs)] if cores == 2 else [])

    widened = hidden.astype(F32)
    inverse_rms = lax.rsqrt(jnp.mean(widened * widened, axis=-1, keepdims=True) + eps_norm)

    def normed_columns(p):
        columns = lax.dynamic_slice_in_dim(hidden, p * part, part, 1).astype(F32)
        gain = lax.dynamic_slice_in_dim(norm_gain, p * part, part, 0).astype(F32)
        return (columns * inverse_rms * gain).astype(BF16)

    normed_own = [normed_columns(p) for p in own_core]

    cut = max(1, (share * 5 // 8) // 16) * 16 if share > 16 else share
    cuts = [(0, cut), (cut, share)] if cut < share else [(0, share)]

    def deal(columns, low, high):
        sent = jnp.dot(
            one_hot_rows(order_grid[:, low:high].reshape(-1), length), columns,
            preferred_element_type=F32,
        ).astype(BF16)
        return lax.all_to_all(sent, "req", split_axis=0, concat_axis=0, tiled=True)

    weights = jnp.concatenate(
        [padded_halves(w_query), padded_halves(w_key), padded_heads(w_value, 1)], axis=1
    )
    weights = jnp.concatenate(
        [lax.dynamic_slice_in_dim(weights, p * part, part, 0) for p in all_pieces], axis=0
    )
    out_weights = [lax.dynamic_slice_in_dim(w_output, p * part, part, 1) for p in all_pieces]
    out_keep = padded_heads(jnp.concatenate(out_weights[:xs], axis=1), 0)
    out_send = padded_heads(jnp.concatenate(out_weights[xs:], axis=1), 0) if cores == 2 else None

    raw_parts = []
    for number, (low, high) in enumerate(cuts):
        if number == 0:
            mine = deal(normed_own[0], low, high)
            mine = jnp.concatenate([mine] + [from_x(mine, k) for k in range(1, xs)], axis=1)
        else:
            mine = deal(jnp.concatenate(normed_own, axis=1), low, high)
        half = mine.shape[1]
        raw = jnp.dot(mine, weights[:half], preferred_element_type=F32)
        if cores == 2:
            other = from_core(mine)
            raw = raw + jnp.dot(other, weights[half:], preferred_element_type=F32)
        raw_parts.append(raw)

    heads_local, kv_local = w_query.shape[1] // HD, w_key.shape[1] // HD
    steps = 2 if share % 32 == 0 else 1
    attended, key_pad, value_pad = attention(
        raw_parts, cuts, groups, heads_local, kv_local, steps, rope_tables(segment_row)
    )

    total = lax.dynamic_slice_in_dim(hidden, tp_place * part, part, 1).astype(F32)
    kept_parts = []
    came_parts = [None] * steps
    if cores == 2:
        came_parts = [
            from_core(jnp.dot(rows, out_send, preferred_element_type=F32).astype(BF16))
            for rows in attended
        ]
    for rows, came in zip(attended, came_parts):
        kept = jnp.dot(rows, out_keep, preferred_element_type=F32)
        kept_parts.append(kept if came is None else kept + came.astype(F32))
    leaving_parts = [
        [kept[:, k * part : (k + 1) * part].astype(BF16) for k in range(1, xs)]
        for kept in kept_parts
    ]
    kept_parts = [kept[:, :part] for kept in kept_parts]
    kept_parts, leaving_parts = lax.optimization_barrier((kept_parts, leaving_parts))
    for step in range(steps):
        low, high = step * share // steps, (step + 1) * share // steps
        summed = kept_parts[step]
        for k in range(1, xs):
            summed = summed + from_x(leaving_parts[step][k - 1], xs - k).astype(F32)
        returned = lax.all_to_all(
            summed.astype(BF16), "req", split_axis=0, concat_axis=0, tiled=True
        )
        back = one_hot_rows(order_grid[:, low:high].reshape(-1), length)
        total = total + lax.dot_general(
            back, returned, (((0,), (0,)), ((), ())), preferred_element_type=F32
        )
    hidden_out = total.astype(BF16)

    pages_dev = length // PAGE
    per_owner = pages_dev // groups
    my_req = lax.axis_index("req")
    owners = page_table // pages_dev
    numbers = jnp.arange(pages_dev, dtype=jnp.int32)
    earlier = (owners[:, None, :] == owners[:, :, None]) & (numbers[None, :] < numbers[:, None])
    rank = jnp.sum(earlier.astype(jnp.int32), axis=-1)
    my_slots = lax.dynamic_slice_in_dim(owners * per_owner + rank, my_req, 1, 0)[0]
    half = HD // 2
    columns = []
    for h in range(kv_local):
        at = h * LANES
        columns += [
            key_pad[:, at : at + half],
            key_pad[:, at + LANES // 2 : at + LANES // 2 + half],
            value_pad[:, at : at + HD],
        ]
    kv_rows = jnp.concatenate(columns, axis=1)
    page_rows = kv_rows.reshape(pages_dev, PAGE * kv_local * 2 * HD)
    page_rows = jnp.dot(
        (my_slots[None, :] == numbers[:, None]).astype(BF16), page_rows,
        preferred_element_type=F32,
    ).astype(BF16)
    arrived = lax.all_to_all(page_rows, "req", split_axis=0, concat_axis=0, tiled=True)
    slot_here = jnp.where(
        owners == my_req, jnp.arange(groups, dtype=jnp.int32)[:, None] * per_owner + rank, -1
    ).reshape(-1)
    target = (page_table % pages_dev).reshape(-1)
    hit = (slot_here[:, None] == numbers[None, :]).astype(jnp.int32)
    slot_target = jnp.sum(hit * target[:, None], axis=0)
    place = (slot_target[None, :] == numbers[:, None]).astype(BF16)
    kv_cache = jnp.dot(place, arrived, preferred_element_type=F32).astype(BF16)
    return (hidden_out, kv_cache.reshape(pages_dev, PAGE, kv_local, 2 * HD))


def solution(mesh):
    return jax.shard_map(
        local,
        mesh=mesh,
        in_specs=(
            P("req", None),
            P("req", None),
            P("req", None),
            P(),
            P(),
            P(None, "tp"),
            P(None, "tp"),
            P(None, "tp"),
            P("tp", None),
        ),
        out_specs=(P("req", "tp"), P("req", None, "tp", None)),
        check_vma=False,
    )
```

```python
import functools
import math

import jax
import jax.numpy as jnp
from jax import lax
from jax.experimental import pallas as pl
from jax.experimental.pallas import tpu as pltpu
from jax.sharding import PartitionSpec as P

HD = 80
PAGE = 16
LONGEST = 512

eps_norm = 1e-05
rope_base = 1000000.0
F32 = jnp.float32
BF16 = jnp.bfloat16


LANES = 128


def padded_halves(array):
    rows = array.shape[0]
    split = array.reshape(rows, -1, 2, HD // 2)
    return jnp.pad(split, ((0, 0), (0, 0), (0, 0), (0, (LANES - HD) // 2))).reshape(rows, -1)


def padded_heads(array, axis):
    shape = array.shape
    split = array.reshape(shape[:axis] + (-1, HD) + shape[axis + 1 :])
    widths = [(0, 0)] * split.ndim
    widths[axis + 1] = (0, LANES - HD)
    return jnp.pad(split, widths).reshape(shape[:axis] + (-1,) + shape[axis + 1 :])


def rope_tables(segment_row):
    length = segment_row.shape[0]
    places = jnp.arange(length, dtype=jnp.int32)
    first_index = jnp.sum((segment_row[None, :] < segment_row[:, None]).astype(jnp.int32), axis=1)
    position = (places - first_index).astype(F32)
    frequency = rope_base ** (-jnp.arange(0, HD, 2, dtype=F32) / HD)
    angles = position[:, None] * frequency[None, :]
    cosine, sine = jnp.cos(angles), jnp.sin(angles)
    cosine = padded_halves(jnp.concatenate([cosine, cosine], axis=-1))
    sine = padded_halves(jnp.concatenate([-sine, sine], axis=-1))
    return cosine, sine, first_index


def attention_kernel(cuts, groups, heads, kv, steps, *refs):
    raw_refs, refs = refs[: len(cuts)], refs[len(cuts) :]
    cos_ref, sin_ref, first_ref = refs[:3]
    out_ref, refs = refs[3], refs[4:]
    key_ref, value_ref, query_scr, value_scr = refs
    share = cuts[-1][1]
    length = groups * share
    scale = math.log2(math.e) / math.sqrt(HD)

    for (low, high), raw_ref in zip(cuts, raw_refs):
        size = high - low

        @pl.loop(0, groups)
        def _(g):
            here = pl.ds(pl.multiple_of(g * size, 16), size)
            there = pl.ds(pl.multiple_of(g * share + low, 16), size)
            cosine, sine = cos_ref[there, :], sin_ref[there, :]
            for h in range(heads + kv):
                x = raw_ref[here, h * LANES : (h + 1) * LANES]
                turned = x * cosine + pltpu.roll(x, LANES // 2, 1) * sine
                if h < heads:
                    query_scr[there, h * LANES : (h + 1) * LANES] = turned.astype(BF16)
                else:
                    at = (h - heads) * LANES
                    key_ref[there, at : at + LANES] = turned.astype(BF16)
            lane = lax.broadcasted_iota(jnp.int32, (size, LANES), 1)
            for h in range(kv):
                at = (heads + kv + h) * LANES
                x = raw_ref[here, at : at + LANES]
                value_ref[there, h * LANES : (h + 1) * LANES] = x.astype(BF16)
                value_scr[there, h * LANES : (h + 1) * LANES] = jnp.where(
                    lane == HD, 1.0, x
                ).astype(BF16)

    tile = 256 if length % 256 == 0 else length
    ratio = heads // kv
    for low in range(0, length, tile):
        high = low + tile
        start = max(0, low - LONGEST)
        keys = high - start
        key_place = start + lax.broadcasted_iota(jnp.int32, (tile, keys), 1)
        query_place = low + lax.broadcasted_iota(jnp.int32, (tile, keys), 0)
        allowed = (key_place >= first_ref[low:high, :]) & (key_place <= query_place)

        @pl.loop(0, heads)
        def _(h):
            mine = pl.ds(pl.multiple_of(h * LANES, LANES), LANES)
            shared = pl.ds(pl.multiple_of((h // ratio) * LANES, LANES), LANES)
            scores = lax.dot_general(
                query_scr[low:high, mine], key_ref[start:high, shared],
                (((1,), (1,)), ((), ())), preferred_element_type=F32,
            )
            probs = jnp.where(allowed, jnp.exp2(scores * scale), 0.0).astype(BF16)
            sums = jnp.dot(probs, value_scr[start:high, shared], preferred_element_type=F32)
            done = (sums / sums[:, HD : HD + 1]).astype(BF16)
            run = share // steps
            for block in range(tile // run):
                g, step = divmod(low // run + block, steps)
                at = (step * groups + g) * run
                out_ref[at : at + run, mine] = done[block * run : (block + 1) * run]


def attention(raw_parts, cuts, groups, heads, kv, steps, tables):
    cosine, sine, first_index = tables
    length = groups * cuts[-1][1]
    shapes = [jax.ShapeDtypeStruct((length, heads * LANES), BF16)]
    shapes += [jax.ShapeDtypeStruct((length, kv * LANES), BF16)] * 2
    whole = pl.BlockSpec(memory_space=pltpu.VMEM)
    outs = pl.pallas_call(
        functools.partial(attention_kernel, cuts, groups, heads, kv, steps),
        out_shape=shapes,
        in_specs=[whole] * (len(cuts) + 3),
        out_specs=[whole] * len(shapes),
        scratch_shapes=[
            pltpu.VMEM((length, heads * LANES), BF16),
            pltpu.VMEM((length, kv * LANES), BF16),
        ],
        compiler_params=pltpu.CompilerParams(vmem_limit_bytes=40 * 2**20),
        cost_estimate=pl.CostEstimate(
            flops=4 * length * 640 * heads * LANES, bytes_accessed=10 * 2**20,
            transcendentals=length * 640 * heads,
        ),
    )(*raw_parts, cosine, sine, first_index[:, None])
    return outs


def return_kernel(
    axes, kept_ref, leaving_ref, order_ref, hidden_ref, out_ref,
    crossed, fin, ret, total, x_send, x_recv, r_send, r_recv,
):
    groups, xs, cores = axes
    steps, _, run, part = kept_ref.shape
    length = out_ref.shape[0]
    me, tp = lax.axis_index("req"), lax.axis_index("tp")
    my_x, my_core = tp // cores, tp % cores

    def group(k):
        return lax.rem(me + k, groups)

    def along_x(k):
        return lax.rem(my_x + k, xs) * cores + my_core

    mesh_ids = pl.DeviceIdType.MESH
    barrier = pltpu.get_barrier_semaphore()

    @pl.loop(1, groups)
    def _(k):
        pl.semaphore_signal(barrier, inc=1, device_id=(group(k), tp), device_id_type=mesh_ids)

    for k in range(1, xs):
        pl.semaphore_signal(barrier, inc=1, device_id=(me, along_x(k)), device_id_type=mesh_ids)
    pl.semaphore_wait(barrier, groups - 1 + xs - 1)

    def x_copy(step, k):
        return pltpu.make_async_remote_copy(
            src_ref=leaving_ref.at[k - 1, step], dst_ref=crossed.at[k - 1, step],
            send_sem=x_send.at[k - 1, step], recv_sem=x_recv.at[k - 1, step],
            device_id=(me, along_x(k)), device_id_type=mesh_ids,
        )

    def ret_copy(step, k):
        return pltpu.make_async_remote_copy(
            src_ref=fin.at[step, group(k)], dst_ref=ret.at[step, me],
            send_sem=r_send.at[step, k], recv_sem=r_recv.at[step, k],
            device_id=(group(k), tp), device_id_type=mesh_ids,
        )

    def ret_arrival(step, k):
        source = group(groups - k)
        return pltpu.make_async_remote_copy(
            src_ref=fin.at[step, source], dst_ref=ret.at[step, source],
            send_sem=r_send.at[step, k], recv_sem=r_recv.at[step, k],
            device_id=(group(k), tp), device_id_type=mesh_ids,
        )

    for step in range(steps):
        for k in range(1, xs):
            x_copy(step, k).start()
    total[...] = hidden_ref[...].astype(F32)

    def take(step):
        @pl.loop(1, groups)
        def _(k):
            ret_arrival(step, k).wait_recv()

        row = lax.broadcasted_iota(jnp.int32, (length, groups * run), 0)
        back = (row == order_ref[step]).astype(F32).astype(BF16)
        arrived = ret[step].reshape(groups * run, part)
        total[...] += jnp.dot(back, arrived, preferred_element_type=F32)

    for step in range(steps):
        summed = kept_ref[step]
        for k in range(1, xs):
            x_copy(step, k).wait_recv()
            summed = summed + crossed[k - 1, step].astype(F32)
        fin[step] = summed.astype(BF16)

        @pl.loop(1, groups)
        def _(k):
            ret_copy(step, k).start()

        ret[step, me] = fin[step, me]
        if step > 0:
            take(step - 1)
    take(steps - 1)
    out_ref[...] = total[...].astype(BF16)

    for step in range(steps):
        for k in range(1, xs):
            x_copy(step, k).wait_send()

        @pl.loop(1, groups)
        def _(k):
            ret_copy(step, k).wait_send()


def give_back(axes, kept, leaving, order, hidden_own):
    groups, xs, _ = axes
    steps, _, run, part = kept.shape
    length = hidden_own.shape[0]
    vmem = pl.BlockSpec(memory_space=pltpu.VMEM)
    dma = pltpu.SemaphoreType.DMA
    return pl.pallas_call(
        functools.partial(return_kernel, axes),
        out_shape=jax.ShapeDtypeStruct((length, part), BF16),
        in_specs=[vmem] * 4,
        out_specs=vmem,
        scratch_shapes=[
            pltpu.VMEM((xs - 1, steps, groups, run, part), BF16),
            pltpu.VMEM((steps, groups, run, part), BF16),
            pltpu.VMEM((steps, groups, run, part), BF16),
            pltpu.VMEM((length, part), F32),
            dma((xs - 1, steps)), dma((xs - 1, steps)),
            dma((steps, groups)), dma((steps, groups)),
        ],
        compiler_params=pltpu.CompilerParams(
            collective_id=0, has_side_effects=True, vmem_limit_bytes=40 * 2**20
        ),
        cost_estimate=pl.CostEstimate(
            flops=2 * length * length * part, bytes_accessed=16 * 2**20, transcendentals=0
        ),
    )(kept, leaving, order, hidden_own)


def one_hot_rows(index, count):
    return (index[:, None] == jnp.arange(count, dtype=jnp.int32)[None, :]).astype(BF16)


def local(hidden, segments, send_order, page_table, norm_gain, w_query, w_key, w_value, w_output):
    groups = lax.axis_size("req")
    tp_count = lax.axis_size("tp")
    length, width = hidden.shape
    share = length // groups
    part = width // tp_count
    cores = 2 if tp_count % 2 == 0 else 1
    xs = tp_count // cores
    tp_place = lax.axis_index("tp")
    my_x, my_core = tp_place // cores, tp_place % cores
    order_grid = send_order[0].reshape(groups, share)
    segment_row = segments[0]

    def piece(k, e):
        return lax.rem(my_x + k, xs) * cores + (my_core ^ e)

    def from_x(array, k):
        pairs = [
            (((x + k) % xs) * cores + c, x * cores + c) for x in range(xs) for c in range(cores)
        ]
        return lax.ppermute(array, "tp", pairs)

    def from_core(array):
        pairs = [(x * cores + (c ^ 1), x * cores + c) for x in range(xs) for c in range(cores)]
        return lax.ppermute(array, "tp", pairs)

    own_core = [piece(k, 0) for k in range(xs)]
    all_pieces = own_core + ([piece(k, 1) for k in range(xs)] if cores == 2 else [])

    widened = hidden.astype(F32)
    inverse_rms = lax.rsqrt(jnp.mean(widened * widened, axis=-1, keepdims=True) + eps_norm)

    def normed_columns(p):
        columns = lax.dynamic_slice_in_dim(hidden, p * part, part, 1).astype(F32)
        gain = lax.dynamic_slice_in_dim(norm_gain, p * part, part, 0).astype(F32)
        return (columns * inverse_rms * gain).astype(BF16)

    normed_own = [normed_columns(p) for p in own_core]

    cut = max(1, (share * 5 // 8) // 16) * 16 if share > 16 else share
    cuts = [(0, cut), (cut, share)] if cut < share else [(0, share)]

    def deal(columns, low, high):
        sent = jnp.dot(
            one_hot_rows(order_grid[:, low:high].reshape(-1), length), columns,
            preferred_element_type=F32,
        ).astype(BF16)
        return lax.all_to_all(sent, "req", split_axis=0, concat_axis=0, tiled=True)

    weights = jnp.concatenate(
        [padded_halves(w_query), padded_halves(w_key), padded_heads(w_value, 1)], axis=1
    )
    weights = jnp.concatenate(
        [lax.dynamic_slice_in_dim(weights, p * part, part, 0) for p in all_pieces], axis=0
    )
    out_weights = [lax.dynamic_slice_in_dim(w_output, p * part, part, 1) for p in all_pieces]
    out_keep = padded_heads(jnp.concatenate(out_weights[:xs], axis=1), 0)
    out_send = padded_heads(jnp.concatenate(out_weights[xs:], axis=1), 0) if cores == 2 else None

    raw_parts = []
    for number, (low, high) in enumerate(cuts):
        if number == 0:
            mine = deal(normed_own[0], low, high)
            mine = jnp.concatenate([mine] + [from_x(mine, k) for k in range(1, xs)], axis=1)
        else:
            mine = deal(jnp.concatenate(normed_own, axis=1), low, high)
        half = mine.shape[1]
        raw = jnp.dot(mine, weights[:half], preferred_element_type=F32)
        if cores == 2:
            other = from_core(mine)
            raw = raw + jnp.dot(other, weights[half:], preferred_element_type=F32)
        raw_parts.append(raw)

    heads_local, kv_local = w_query.shape[1] // HD, w_key.shape[1] // HD
    steps = 4 if share % 64 == 0 else 2 if share % 32 == 0 else 1
    attended, key_pad, value_pad = attention(
        raw_parts, cuts, groups, heads_local, kv_local, steps, rope_tables(segment_row)
    )

    run = share // steps
    kept = jnp.dot(attended, out_keep, preferred_element_type=F32)
    if cores == 2:
        given = jnp.dot(attended, out_send, preferred_element_type=F32).astype(BF16)
        kept = kept + from_core(given).astype(F32)
    kept = kept.reshape(steps, groups, run, -1)
    leaving = [kept[..., k * part : (k + 1) * part].astype(BF16) for k in range(1, xs)]
    order_steps = order_grid.reshape(groups, steps, run).transpose(1, 0, 2)
    hidden_out = give_back(
        (groups, xs, cores), kept[..., :part], jnp.stack(leaving),
        order_steps.reshape(steps, 1, groups * run),
        lax.dynamic_slice_in_dim(hidden, tp_place * part, part, 1),
    )

    pages_dev = length // PAGE
    per_owner = pages_dev // groups
    my_req = lax.axis_index("req")
    owners = page_table // pages_dev
    numbers = jnp.arange(pages_dev, dtype=jnp.int32)
    earlier = (owners[:, None, :] == owners[:, :, None]) & (numbers[None, :] < numbers[:, None])
    rank = jnp.sum(earlier.astype(jnp.int32), axis=-1)
    my_slots = lax.dynamic_slice_in_dim(owners * per_owner + rank, my_req, 1, 0)[0]
    half = HD // 2
    columns = []
    for h in range(kv_local):
        at = h * LANES
        columns += [
            key_pad[:, at : at + half],
            key_pad[:, at + LANES // 2 : at + LANES // 2 + half],
            value_pad[:, at : at + HD],
        ]
    kv_rows = jnp.concatenate(columns, axis=1)
    page_rows = kv_rows.reshape(pages_dev, PAGE * kv_local * 2 * HD)
    page_rows = jnp.dot(
        (my_slots[None, :] == numbers[:, None]).astype(BF16), page_rows,
        preferred_element_type=F32,
    ).astype(BF16)
    arrived = lax.all_to_all(page_rows, "req", split_axis=0, concat_axis=0, tiled=True)
    slot_here = jnp.where(
        owners == my_req, jnp.arange(groups, dtype=jnp.int32)[:, None] * per_owner + rank, -1
    ).reshape(-1)
    target = (page_table % pages_dev).reshape(-1)
    hit = (slot_here[:, None] == numbers[None, :]).astype(jnp.int32)
    slot_target = jnp.sum(hit * target[:, None], axis=0)
    place = (slot_target[None, :] == numbers[:, None]).astype(BF16)
    kv_cache = jnp.dot(place, arrived, preferred_element_type=F32).astype(BF16)
    return (hidden_out, kv_cache.reshape(pages_dev, PAGE, kv_local, 2 * HD))


def solution(mesh):
    return jax.shard_map(
        local,
        mesh=mesh,
        in_specs=(
            P("req", None),
            P("req", None),
            P("req", None),
            P(),
            P(),
            P(None, "tp"),
            P(None, "tp"),
            P(None, "tp"),
            P("tp", None),
        ),
        out_specs=(P("req", "tp"), P("req", None, "tp", None)),
        check_vma=False,
    )
```

```python
import functools
import math

import jax
import jax.numpy as jnp
from jax import lax
from jax.experimental import pallas as pl
from jax.experimental.pallas import tpu as pltpu
from jax.sharding import PartitionSpec as P

HD = 80
PAGE = 16
LONGEST = 512

eps_norm = 1e-05
rope_base = 1000000.0
F32 = jnp.float32
BF16 = jnp.bfloat16


LANES = 128


def padded_halves(array):
    rows = array.shape[0]
    split = array.reshape(rows, -1, 2, HD // 2)
    return jnp.pad(split, ((0, 0), (0, 0), (0, 0), (0, (LANES - HD) // 2))).reshape(rows, -1)


def padded_heads(array, axis):
    shape = array.shape
    split = array.reshape(shape[:axis] + (-1, HD) + shape[axis + 1 :])
    widths = [(0, 0)] * split.ndim
    widths[axis + 1] = (0, LANES - HD)
    return jnp.pad(split, widths).reshape(shape[:axis] + (-1,) + shape[axis + 1 :])


def rope_tables(segment_row):
    length = segment_row.shape[0]
    places = jnp.arange(length, dtype=jnp.int32)
    first_index = jnp.sum((segment_row[None, :] < segment_row[:, None]).astype(jnp.int32), axis=1)
    position = (places - first_index).astype(F32)
    frequency = rope_base ** (-jnp.arange(0, HD, 2, dtype=F32) / HD)
    angles = position[:, None] * frequency[None, :]
    cosine, sine = jnp.cos(angles), jnp.sin(angles)
    cosine = padded_halves(jnp.concatenate([cosine, cosine], axis=-1))
    sine = padded_halves(jnp.concatenate([-sine, sine], axis=-1))
    return cosine, sine, first_index


def attention_kernel(cuts, groups, heads, kv, steps, *refs):
    raw_refs, refs = refs[: len(cuts)], refs[len(cuts) :]
    cos_ref, sin_ref, first_ref = refs[:3]
    out_ref, refs = refs[3], refs[4:]
    key_ref, value_ref, query_scr, value_scr = refs
    share = cuts[-1][1]
    length = groups * share
    scale = math.log2(math.e) / math.sqrt(HD)

    for (low, high), raw_ref in zip(cuts, raw_refs):
        size = high - low

        @pl.loop(0, groups)
        def _(g):
            here = pl.ds(pl.multiple_of(g * size, 16), size)
            there = pl.ds(pl.multiple_of(g * share + low, 16), size)
            cosine, sine = cos_ref[there, :], sin_ref[there, :]
            for h in range(heads + kv):
                x = raw_ref[here, h * LANES : (h + 1) * LANES]
                turned = x * cosine + pltpu.roll(x, LANES // 2, 1) * sine
                if h < heads:
                    query_scr[there, h * LANES : (h + 1) * LANES] = turned.astype(BF16)
                else:
                    at = (h - heads) * LANES
                    key_ref[there, at : at + LANES] = turned.astype(BF16)
            lane = lax.broadcasted_iota(jnp.int32, (size, LANES), 1)
            for h in range(kv):
                at = (heads + kv + h) * LANES
                x = raw_ref[here, at : at + LANES]
                value_ref[there, h * LANES : (h + 1) * LANES] = x.astype(BF16)
                value_scr[there, h * LANES : (h + 1) * LANES] = jnp.where(
                    lane == HD, 1.0, x
                ).astype(BF16)

    tile = 256 if length % 256 == 0 else length
    ratio = heads // kv
    for low in range(0, length, tile):
        high = low + tile
        start = max(0, low - LONGEST)
        keys = high - start
        key_place = start + lax.broadcasted_iota(jnp.int32, (tile, keys), 1)
        query_place = low + lax.broadcasted_iota(jnp.int32, (tile, keys), 0)
        allowed = (key_place >= first_ref[low:high, :]) & (key_place <= query_place)

        @pl.loop(0, heads)
        def _(h):
            mine = pl.ds(pl.multiple_of(h * LANES, LANES), LANES)
            shared = pl.ds(pl.multiple_of((h // ratio) * LANES, LANES), LANES)
            scores = lax.dot_general(
                query_scr[low:high, mine], key_ref[start:high, shared],
                (((1,), (1,)), ((), ())), preferred_element_type=F32,
            )
            probs = jnp.where(allowed, jnp.exp2(scores * scale), 0.0).astype(BF16)
            sums = jnp.dot(probs, value_scr[start:high, shared], preferred_element_type=F32)
            done = (sums / sums[:, HD : HD + 1]).astype(BF16)
            run = share // steps
            for block in range(tile // run):
                g, step = divmod(low // run + block, steps)
                at = (step * groups + g) * run
                out_ref[at : at + run, mine] = done[block * run : (block + 1) * run]


def attention(raw_parts, cuts, groups, heads, kv, steps, tables):
    cosine, sine, first_index = tables
    length = groups * cuts[-1][1]
    shapes = [jax.ShapeDtypeStruct((length, heads * LANES), BF16)]
    shapes += [jax.ShapeDtypeStruct((length, kv * LANES), BF16)] * 2
    whole = pl.BlockSpec(memory_space=pltpu.VMEM)
    outs = pl.pallas_call(
        functools.partial(attention_kernel, cuts, groups, heads, kv, steps),
        out_shape=shapes,
        in_specs=[whole] * (len(cuts) + 3),
        out_specs=[whole] * len(shapes),
        scratch_shapes=[
            pltpu.VMEM((length, heads * LANES), BF16),
            pltpu.VMEM((length, kv * LANES), BF16),
        ],
        compiler_params=pltpu.CompilerParams(vmem_limit_bytes=40 * 2**20),
        cost_estimate=pl.CostEstimate(
            flops=4 * length * 640 * heads * LANES, bytes_accessed=10 * 2**20,
            transcendentals=length * 640 * heads,
        ),
    )(*raw_parts, cosine, sine, first_index[:, None])
    return outs


def return_kernel(
    axes, kept_ref, leaving_ref, order_ref, hidden_ref, page_ref, place_ref, out_ref, cache_ref,
    pages, p_send, p_recv, crossed, fin, ret, total, x_send, x_recv, r_send, r_recv,
):
    groups, xs, cores = axes
    steps, _, run, part = kept_ref.shape
    length = out_ref.shape[0]
    me, tp = lax.axis_index("req"), lax.axis_index("tp")
    my_x, my_core = tp // cores, tp % cores

    def group(k):
        return lax.rem(me + k, groups)

    def along_x(k):
        return lax.rem(my_x + k, xs) * cores + my_core

    mesh_ids = pl.DeviceIdType.MESH
    barrier = pltpu.get_barrier_semaphore()

    @pl.loop(1, groups)
    def _(k):
        pl.semaphore_signal(barrier, inc=1, device_id=(group(k), tp), device_id_type=mesh_ids)

    for k in range(1, xs):
        pl.semaphore_signal(barrier, inc=1, device_id=(me, along_x(k)), device_id_type=mesh_ids)
    pl.semaphore_wait(barrier, groups - 1 + xs - 1)

    def x_copy(step, k):
        return pltpu.make_async_remote_copy(
            src_ref=leaving_ref.at[k - 1, step], dst_ref=crossed.at[k - 1, step],
            send_sem=x_send.at[k - 1, step], recv_sem=x_recv.at[k - 1, step],
            device_id=(me, along_x(k)), device_id_type=mesh_ids,
        )

    def ret_copy(step, k):
        return pltpu.make_async_remote_copy(
            src_ref=fin.at[step, group(k)], dst_ref=ret.at[step, me],
            send_sem=r_send.at[step, k], recv_sem=r_recv.at[step, k],
            device_id=(group(k), tp), device_id_type=mesh_ids,
        )

    def ret_arrival(step, k):
        source = group(groups - k)
        return pltpu.make_async_remote_copy(
            src_ref=fin.at[step, source], dst_ref=ret.at[step, source],
            send_sem=r_send.at[step, k], recv_sem=r_recv.at[step, k],
            device_id=(group(k), tp), device_id_type=mesh_ids,
        )

    def page_copy(k):
        return pltpu.make_async_remote_copy(
            src_ref=page_ref.at[group(k)], dst_ref=pages.at[me],
            send_sem=p_send.at[k], recv_sem=p_recv.at[k],
            device_id=(group(k), tp), device_id_type=mesh_ids,
        )

    def page_arrival(k):
        source = group(groups - k)
        return pltpu.make_async_remote_copy(
            src_ref=page_ref.at[source], dst_ref=pages.at[source],
            send_sem=p_send.at[k], recv_sem=p_recv.at[k],
            device_id=(group(k), tp), device_id_type=mesh_ids,
        )

    for step in range(steps):
        for k in range(1, xs):
            x_copy(step, k).start()

    @pl.loop(1, groups)
    def _(k):
        page_copy(k).start()

    pages[me] = page_ref[me]
    total[...] = hidden_ref[...].astype(F32)

    def take(step):
        @pl.loop(1, groups)
        def _(k):
            ret_arrival(step, k).wait_recv()

        row = lax.broadcasted_iota(jnp.int32, (length, groups * run), 0)
        back = (row == order_ref[step]).astype(F32).astype(BF16)
        arrived = ret[step].reshape(groups * run, part)
        total[...] += jnp.dot(back, arrived, preferred_element_type=F32)

    for step in range(steps):
        summed = kept_ref[step]
        for k in range(1, xs):
            x_copy(step, k).wait_recv()
            summed = summed + crossed[k - 1, step].astype(F32)
        fin[step] = summed.astype(BF16)

        @pl.loop(1, groups)
        def _(k):
            ret_copy(step, k).start()

        ret[step, me] = fin[step, me]
        if step > 0:
            take(step - 1)

    @pl.loop(1, groups)
    def _(k):
        page_arrival(k).wait_recv()

    row = lax.broadcasted_iota(jnp.int32, (length, length), 0)
    place = (row == place_ref[...]).astype(F32).astype(BF16)
    rows = pages[...].reshape(length, pages.shape[-1])
    cache_ref[...] = jnp.dot(place, rows, preferred_element_type=F32).astype(BF16)
    take(steps - 1)
    out_ref[...] = total[...].astype(BF16)

    @pl.loop(1, groups)
    def _(k):
        page_copy(k).wait_send()

    for step in range(steps):
        for k in range(1, xs):
            x_copy(step, k).wait_send()

        @pl.loop(1, groups)
        def _(k):
            ret_copy(step, k).wait_send()


def give_back(axes, kept, leaving, order, hidden_own, page_rows, place):
    groups, xs, _ = axes
    steps, _, run, part = kept.shape
    length = hidden_own.shape[0]
    vmem = pl.BlockSpec(memory_space=pltpu.VMEM)
    dma = pltpu.SemaphoreType.DMA
    return pl.pallas_call(
        functools.partial(return_kernel, axes),
        out_shape=[
            jax.ShapeDtypeStruct((length, part), BF16),
            jax.ShapeDtypeStruct((length, page_rows.shape[-1]), BF16),
        ],
        in_specs=[vmem] * 6,
        out_specs=[vmem] * 2,
        scratch_shapes=[
            pltpu.VMEM(page_rows.shape, BF16), dma((groups,)), dma((groups,)),
            pltpu.VMEM((xs - 1, steps, groups, run, part), BF16),
            pltpu.VMEM((steps, groups, run, part), BF16),
            pltpu.VMEM((steps, groups, run, part), BF16),
            pltpu.VMEM((length, part), F32),
            dma((xs - 1, steps)), dma((xs - 1, steps)),
            dma((steps, groups)), dma((steps, groups)),
        ],
        compiler_params=pltpu.CompilerParams(
            collective_id=0, has_side_effects=True, vmem_limit_bytes=40 * 2**20
        ),
        cost_estimate=pl.CostEstimate(
            flops=2 * length * length * part, bytes_accessed=16 * 2**20, transcendentals=0
        ),
    )(kept, leaving, order, hidden_own, page_rows, place)


def one_hot_rows(index, count):
    return (index[:, None] == jnp.arange(count, dtype=jnp.int32)[None, :]).astype(BF16)


def local(hidden, segments, send_order, page_table, norm_gain, w_query, w_key, w_value, w_output):
    groups = lax.axis_size("req")
    tp_count = lax.axis_size("tp")
    length, width = hidden.shape
    share = length // groups
    part = width // tp_count
    cores = 2 if tp_count % 2 == 0 else 1
    xs = tp_count // cores
    tp_place = lax.axis_index("tp")
    my_x, my_core = tp_place // cores, tp_place % cores
    order_grid = send_order[0].reshape(groups, share)
    segment_row = segments[0]

    def piece(k, e):
        return lax.rem(my_x + k, xs) * cores + (my_core ^ e)

    def from_x(array, k):
        pairs = [
            (((x + k) % xs) * cores + c, x * cores + c) for x in range(xs) for c in range(cores)
        ]
        return lax.ppermute(array, "tp", pairs)

    def from_core(array):
        pairs = [(x * cores + (c ^ 1), x * cores + c) for x in range(xs) for c in range(cores)]
        return lax.ppermute(array, "tp", pairs)

    own_core = [piece(k, 0) for k in range(xs)]
    all_pieces = own_core + ([piece(k, 1) for k in range(xs)] if cores == 2 else [])

    widened = hidden.astype(F32)
    inverse_rms = lax.rsqrt(jnp.mean(widened * widened, axis=-1, keepdims=True) + eps_norm)

    def normed_columns(p):
        columns = lax.dynamic_slice_in_dim(hidden, p * part, part, 1).astype(F32)
        gain = lax.dynamic_slice_in_dim(norm_gain, p * part, part, 0).astype(F32)
        return (columns * inverse_rms * gain).astype(BF16)

    normed_own = [normed_columns(p) for p in own_core]

    cut = max(1, (share * 5 // 8) // 16) * 16 if share > 16 else share
    cuts = [(0, cut), (cut, share)] if cut < share else [(0, share)]

    def deal(columns, low, high):
        sent = jnp.dot(
            one_hot_rows(order_grid[:, low:high].reshape(-1), length), columns,
            preferred_element_type=F32,
        ).astype(BF16)
        return lax.all_to_all(sent, "req", split_axis=0, concat_axis=0, tiled=True)

    weights = jnp.concatenate(
        [padded_halves(w_query), padded_halves(w_key), padded_heads(w_value, 1)], axis=1
    )
    weights = jnp.concatenate(
        [lax.dynamic_slice_in_dim(weights, p * part, part, 0) for p in all_pieces], axis=0
    )
    out_weights = [lax.dynamic_slice_in_dim(w_output, p * part, part, 1) for p in all_pieces]
    out_keep = padded_heads(jnp.concatenate(out_weights[:xs], axis=1), 0)
    out_send = padded_heads(jnp.concatenate(out_weights[xs:], axis=1), 0) if cores == 2 else None

    raw_parts = []
    for number, (low, high) in enumerate(cuts):
        if number == 0:
            mine = deal(normed_own[0], low, high)
            mine = jnp.concatenate([mine] + [from_x(mine, k) for k in range(1, xs)], axis=1)
        else:
            mine = deal(jnp.concatenate(normed_own, axis=1), low, high)
        half = mine.shape[1]
        raw = jnp.dot(mine, weights[:half], preferred_element_type=F32)
        if cores == 2:
            other = from_core(mine)
            raw = raw + jnp.dot(other, weights[half:], preferred_element_type=F32)
        raw_parts.append(raw)

    heads_local, kv_local = w_query.shape[1] // HD, w_key.shape[1] // HD
    steps = 4 if share % 64 == 0 else 2 if share % 32 == 0 else 1
    attended, key_pad, value_pad = attention(
        raw_parts, cuts, groups, heads_local, kv_local, steps, rope_tables(segment_row)
    )

    run = share // steps
    kept = jnp.dot(attended, out_keep, preferred_element_type=F32)
    if cores == 2:
        given = jnp.dot(attended, out_send, preferred_element_type=F32).astype(BF16)
        kept = kept + from_core(given).astype(F32)
    kept = kept.reshape(steps, groups, run, -1)
    leaving = [kept[..., k * part : (k + 1) * part].astype(BF16) for k in range(1, xs)]
    order_steps = order_grid.reshape(groups, steps, run).transpose(1, 0, 2)
    pages_dev = length // PAGE
    per_owner = pages_dev // groups
    my_req = lax.axis_index("req")
    owners = page_table // pages_dev
    numbers = jnp.arange(pages_dev, dtype=jnp.int32)
    earlier = (owners[:, None, :] == owners[:, :, None]) & (numbers[None, :] < numbers[:, None])
    rank = jnp.sum(earlier.astype(jnp.int32), axis=-1)
    my_slots = lax.dynamic_slice_in_dim(owners * per_owner + rank, my_req, 1, 0)[0]
    half = HD // 2
    columns = []
    for h in range(kv_local):
        at = h * LANES
        columns += [
            key_pad[:, at : at + half],
            key_pad[:, at + LANES // 2 : at + LANES // 2 + half],
            value_pad[:, at : at + HD],
        ]
    kv_rows = jnp.concatenate(columns, axis=1)
    tokens = jnp.arange(PAGE, dtype=jnp.int32)[None, :]
    row_slots = (my_slots[:, None] * PAGE + tokens).reshape(-1)
    row_numbers = jnp.arange(length, dtype=jnp.int32)
    page_rows = jnp.dot(
        (row_slots[None, :] == row_numbers[:, None]).astype(BF16), kv_rows,
        preferred_element_type=F32,
    ).astype(BF16).reshape(groups, share, -1)
    slot_here = jnp.where(
        owners == my_req, jnp.arange(groups, dtype=jnp.int32)[:, None] * per_owner + rank, -1
    ).reshape(-1)
    target = (page_table % pages_dev).reshape(-1)
    hit = (slot_here[:, None] == numbers[None, :]).astype(jnp.int32)
    slot_target = jnp.sum(hit * target[:, None], axis=0)
    place = (slot_target[:, None] * PAGE + tokens).reshape(1, -1)

    hidden_out, kv_cache = give_back(
        (groups, xs, cores), kept[..., :part], jnp.stack(leaving),
        order_steps.reshape(steps, 1, groups * run),
        lax.dynamic_slice_in_dim(hidden, tp_place * part, part, 1),
        page_rows, place,
    )
    return (hidden_out, kv_cache.reshape(pages_dev, PAGE, kv_local, 2 * HD))


def solution(mesh):
    return jax.shard_map(
        local,
        mesh=mesh,
        in_specs=(
            P("req", None),
            P("req", None),
            P("req", None),
            P(),
            P(),
            P(None, "tp"),
            P(None, "tp"),
            P(None, "tp"),
            P("tp", None),
        ),
        out_specs=(P("req", "tp"), P("req", None, "tp", None)),
        check_vma=False,
    )
```
